32 devices in a mesh: group: 2 (over y), blk: 4 (over z), own: 4 (over x, core).
Axes of the slice: x: 2, y: 2, z: 4, core: 2. Of those that a mesh axis runs over, the one named last changes fastest.
Arguments:
- activations: bfloat16 [1, 1024, 28672], P(None, ('group', 'blk'), 'own'), parts along dimension 1, may hold values from -6 to 6
- rank_grads: bfloat16 [1, 1024, 16], P(None, ('group', 'blk')), parts along dimension 1, may hold values from -1.1953125 to 1.1953125
- lengths: int32 [1, 8, 2], P(None, ('group', 'blk')), parts along dimension 1, may hold values from 1 to 96, 128 in all within a row
- adapter_ids: int32 [1, 16], P(None, 'group'), parts along dimension 1, may hold values from 0 to 3, as said below
- input_basis: bfloat16 [128, 28672], P(('group', 'blk'), 'own'), parts along dimension 0, may hold values from -0.03125 to 0.03125
- rank_basis: float32 [8, 16, 16], P('group'), parts along dimension 0, may hold values from -1.5 to 1.5
- prior_values: float32 [8, 16, 64], P('group', None, ('blk', 'own')), parts along dimension 0, may hold values from 0.5 to 4
Outputs:
- eigenvalues: float32 [8, 16, 64], P('group', None, ('blk', 'own')), parts along dimension 0
The draws below stay inside these ranges and needn't reach their ends.
There are 2 independent parts, one for each index of `group`. The reference program is written for one: setup_inputs(seed, part) draws one part's arguments, and reference() takes and returns one part's arrays. A program takes and returns all parts, laid end to end along the dimension named above; each array names one. Nothing has to cross between parts.
Inputs may be any that keep to these rules, and one draw needn't show every extreme that they name: `adapter_ids`: every one of the 4 adapters names at least one sequence of every step.
All inputs are finite; a program needn't handle non-finite values.
Results may differ from the reference program's by a relative error of at most 0.0003.
Values may be sent and summed in bfloat16 or wider, within the bound.
A program may use at most 128 MiB of HBM per device.

```python
import math
import jax
import jax.numpy as jnp
import numpy as np
from jax import lax

DIN = 28672
RANK = 16
ADAPTERS = 4
STEPS = 1
TOK_DEV = 128
SEQ_DEV = 2
SHARDS = 4
TOKENS = 512
SEQS = 8
EIG = 64


def draw_adapter_ids(key, part):
    key = jax.random.fold_in(key, 11)

    def draw_step(step_key):
        key_extra, key_order = jax.random.split(step_key)
        extra_ids = jax.random.randint(key_extra, (SEQS - ADAPTERS,), 0, ADAPTERS, dtype=jnp.int32)
        base_ids = jnp.concatenate([jnp.arange(ADAPTERS, dtype=jnp.int32), extra_ids])
        return jax.random.permutation(key_order, base_ids)
    return jax.vmap(draw_step)(jax.random.split(key, STEPS))


def steps_of(key, dims, cuts, smallest, high):
    def one(position, shards_of):
        draws = jax.random.uniform(jax.random.fold_in(jax.random.fold_in(key, 6), position), (shards_of,), jnp.float32, smallest / len(cuts), high / len(cuts))
        return jnp.repeat(jnp.exp(draws), dims[position] // shards_of).reshape((-1,) + (1,) * (len(dims) - position - 1))

    level = one(*cuts[0])
    for cut in cuts[1:]:
        level = level * one(*cut)
    return level


def length_profile(number_of, total, bound, lean):
    weights = [(1 << 20) // math.isqrt(rank ** lean) + 1 for rank in range(2, number_of + 1)]
    rest, holding = total - bound - (number_of - 1), [1] * (number_of - 1)
    while rest > 0:
        free = [i for i in range(number_of - 1) if holding[i] < bound]
        whole, budget = sum([weights[i] for i in free]), rest
        for i in free:
            addition = min(bound - holding[i], max(1, budget * weights[i] // whole), rest)
            holding[i] = holding[i] + addition
            rest = rest - addition
    return np.array([bound] + holding)


def uneven(stream_key, number_of, total, limit, lean):
    if number_of == 2:
        one = jax.random.randint(stream_key, (), max(1, total - limit), min(limit, total - 1) + 1)
        return jnp.stack([one, total - one])
    sizes = jnp.asarray(length_profile(number_of, total, limit, lean), jnp.int32)
    pairs = (number_of - 1) // 2
    donor, sink = sizes[1:1 + 2 * pairs:2], sizes[2:2 + 2 * pairs:2]
    margin = jnp.minimum(donor - 1, limit - sink)
    shifted = jax.random.randint(jax.random.fold_in(stream_key, 1), (pairs,), 0, 1 << 20) % (margin + 1)
    sizes = sizes.at[1:1 + 2 * pairs:2].set(donor - shifted).at[2:2 + 2 * pairs:2].set(sink + shifted)
    return sizes[jax.random.permutation(jax.random.fold_in(stream_key, 2), number_of)]


def gaussian(own_key, dims, scale, reach, cuts=(), kind=jnp.bfloat16):
    level = steps_of(own_key, dims, cuts, -0.22, 0.18) if cuts else 1.0
    array = jax.random.normal(own_key, dims, jnp.float32) * scale * level
    return jnp.minimum(jnp.maximum(array, -reach), reach).astype(kind)


def setup_inputs(seed: int = 0, part: int = 0) -> dict:
    splits = jax.random.split(jax.random.key(seed), 8)
    own_keys = jax.random.split(jax.random.fold_in(splits[7], part), 8)
    return {
        "activations": gaussian(own_keys[0], (STEPS, TOKENS, DIN), 1.0, 6.0, ((1, 4), (2, 4))),
        "rank_grads": gaussian(own_keys[1], (STEPS, TOKENS, RANK), 0.2, 1.1953125, ((1, 4),)),
        "lengths": jax.vmap(lambda own: uneven(own, SEQ_DEV, TOK_DEV, TOK_DEV * 3 // 4, 1))(jax.random.split(own_keys[2], STEPS * SHARDS)).reshape((STEPS, SHARDS, SEQ_DEV)).astype(jnp.int32),
        "adapter_ids": draw_adapter_ids(jax.random.fold_in(jax.random.fold_in(splits[7], part), 71), part),
        "input_basis": gaussian(own_keys[4], (EIG, DIN), DIN ** -0.5, 0.03125, ((0, 4), (1, 4))),
        "rank_basis": gaussian(own_keys[5], (ADAPTERS, RANK, RANK), RANK ** -0.5, 1.5, (), jnp.float32),
        "prior_values": jnp.clip(jnp.exp(math.log(4.0) - 2.0794415 * jax.random.uniform(own_keys[6], (ADAPTERS, RANK, EIG), jnp.float32) ** steps_of(own_keys[6], (ADAPTERS, RANK, EIG), ((2, 16),), -0.2, 0.2)), 0.5, 4.0),
    }


forget_rate = 0.5


def rank_weights(rank_grads, lengths, local_ids, rank_basis):
    token_count = rank_grads.shape[1]
    adapter_count = rank_basis.shape[0]
    seq_ends = jnp.cumsum(lengths, axis=1)
    starts = seq_ends - lengths
    positions = jnp.arange(token_count, dtype=jnp.int32)
    member = ((positions >= starts[..., None]) & (positions < seq_ends[..., None])).astype(jnp.float32)
    onehot = (local_ids[..., None] == jnp.arange(adapter_count, dtype=jnp.int32)).astype(jnp.float32)
    seq_basis = jnp.einsum('sna,aqr->snqr', onehot, rank_basis, precision=lax.Precision.HIGHEST)
    projected = jnp.einsum('stq,snqr->snrt', rank_grads.astype(jnp.float32), seq_basis, precision=lax.Precision.HIGHEST)
    return projected * member[:, :, None, :]


def reference(activations, rank_grads, lengths, adapter_ids, input_basis, rank_basis, prior_values):
    basis_full = input_basis.astype(jnp.float32)
    accumulated = prior_values * (forget_rate ** STEPS)
    adapter_range = jnp.arange(ADAPTERS, dtype=jnp.int32)
    for step_index in range(STEPS):
        onehot = (adapter_ids[step_index][:, None] == adapter_range).astype(jnp.float32)
        counts = jnp.sum(onehot, axis=0)
        step_grads = rank_grads[step_index].reshape(SHARDS, TOK_DEV, RANK)
        step_acts = activations[step_index].reshape(SHARDS, TOK_DEV, DIN)
        step_ids = adapter_ids[step_index].reshape(SHARDS, SEQ_DEV)
        weights = rank_weights(step_grads, lengths[step_index], step_ids, rank_basis)

        def group_shard(shard_pair):
            shard_weights, shard_acts = shard_pair
            return jnp.einsum('nrt,td->nrd', shard_weights, shard_acts.astype(jnp.float32), precision=lax.Precision.HIGHEST)

        grouped = lax.map(group_shard, (weights, step_acts))
        rotated = jnp.dot(grouped.reshape(SEQS * RANK, DIN), basis_full.T, precision=lax.Precision.HIGHEST)
        squares = (rotated * rotated).reshape(SEQS, RANK, EIG)
        mean_sq = jnp.einsum('na,nrc->arc', onehot / counts, squares, precision=lax.Precision.HIGHEST)
        accumulated = accumulated + (1.0 - forget_rate) * (forget_rate ** (STEPS - 1 - step_index)) * mean_sq
    return accumulated
```

```python
import functools

import jax
import jax.numpy as jnp
from jax import lax
from jax.experimental import pallas as pl
from jax.experimental.pallas import tpu as pltpu
from jax.sharding import PartitionSpec as P

forget_rate = 0.5
HIGHEST = lax.Precision.HIGHEST
MESH = pl.DeviceIdType.MESH


def kernel(
    n, own_n, chunks,
    lengths, ids, acts_hbm, grads, basis_hbm, rank_basis, out,
    acts, panel, rot, part, part_in, sq, sq_in, load_sem, rs, rr, ls, lr, s1, r1, s2, r2,
):
    z = lax.axis_index("blk")
    o = lax.axis_index("own")
    tokens, width = acts.shape
    cols = panel.shape[1]
    share = cols // own_n
    wide = width // chunks
    seqs = lengths.shape[2]
    adapters, rank = rank_basis.shape[0], rank_basis.shape[1]
    lanes = seqs * adapters * rank
    half = adapters * rank

    load_acts = pltpu.make_async_copy(acts_hbm.at[0], acts, load_sem.at[0])
    load_acts.start()
    load_own = pltpu.make_async_copy(basis_hbm, panel.at[z], load_sem.at[1])
    load_own.start()

    barrier = pltpu.get_barrier_semaphore()

    def greet_blk(k, carry):
        pl.semaphore_signal(
            barrier, inc=1, device_id={"blk": lax.rem(z + k, n)}, device_id_type=MESH
        )
        return carry

    lax.fori_loop(1, n, greet_blk, 0)
    for k in range(1, own_n):
        pl.semaphore_signal(
            barrier, inc=1, device_id={"own": lax.rem(o + k, own_n)}, device_id_type=MESH
        )
    pl.semaphore_wait(barrier, n - 1 + own_n - 1)

    def piece(c):
        return pl.ds(c * wide, wide)

    def right(s, c, first=False):
        at = (slice(None), piece(c))
        block = z - s
        return pltpu.make_async_remote_copy(
            src_ref=basis_hbm.at[at] if first else panel.at[(block,) + at],
            dst_ref=panel.at[(block,) + at],
            send_sem=rs.at[s, c], recv_sem=rr.at[s, c],
            device_id={"blk": z + 1}, device_id_type=MESH,
        )

    def left(s, c, first=False):
        at = (slice(None), piece(c))
        block = z + s
        return pltpu.make_async_remote_copy(
            src_ref=basis_hbm.at[at] if first else panel.at[(block,) + at],
            dst_ref=panel.at[(block,) + at],
            send_sem=ls.at[s, c], recv_sem=lr.at[s, c],
            device_id={"blk": z - 1}, device_id_type=MESH,
        )

    def from_left(s, c):
        dst = panel.at[z - 1 - s, :, piece(c)]
        return pltpu.make_async_remote_copy(
            src_ref=dst, dst_ref=dst, send_sem=rs.at[s, c], recv_sem=rr.at[s, c],
            device_id={"blk": z - 1}, device_id_type=MESH,
        )

    def from_right(s, c):
        dst = panel.at[z + 1 + s, :, piece(c)]
        return pltpu.make_async_remote_copy(
            src_ref=dst, dst_ref=dst, send_sem=ls.at[s, c], recv_sem=lr.at[s, c],
            device_id={"blk": z + 1}, device_id_type=MESH,
        )

    for c in range(chunks):
        @pl.when(z < n - 1)
        def _():
            right(0, c, True).start()

        @pl.when(z > 0)
        def _():
            left(0, c, True).start()

    lane = lax.broadcasted_iota(jnp.int32, (1, lanes), 1)
    lane_seq = lane // half
    lane_adapter = lax.rem(lane // rank, adapters)
    lane_id = jnp.zeros((1, lanes), jnp.int32)
    lane_start = jnp.zeros((1, lanes), jnp.int32)
    lane_end = jnp.zeros((1, lanes), jnp.int32)
    start = jnp.int32(0)
    for q in range(seqs):
        end = start + lengths[0, 0, q]
        here = lane_seq == q
        lane_id = jnp.where(here, ids[0, z * seqs + q], lane_id)
        lane_start = jnp.where(here, start, lane_start)
        lane_end = jnp.where(here, end, lane_end)
        start = end

    def count(k, total):
        return total + jnp.where(lane_adapter == ids[0, k], 1.0, 0.0)

    counts = lax.fori_loop(0, ids.shape[1], count, jnp.zeros((1, lanes), jnp.float32))
    scale = (1.0 - forget_rate) / counts
    spread = jnp.concatenate([rank_basis[a] for a in range(adapters)] * seqs, axis=1)
    spread = jnp.where(lane_id == lane_adapter, spread, 0.0)
    weights = jnp.dot(
        grads[0].astype(jnp.float32), spread, precision=HIGHEST,
        preferred_element_type=jnp.float32,
    )
    token = lax.broadcasted_iota(jnp.int32, (tokens, lanes), 0)
    weights = jnp.where((token >= lane_start) & (token < lane_end), weights, 0.0)

    def rotate(block, c):
        return lax.dot_general(
            acts[:, c * wide:(c + 1) * wide], panel[block, :, c * wide:(c + 1) * wide],
            (((1,), (1,)), ((), ())), preferred_element_type=jnp.float32,
        )

    def add(block, c):
        value = rotate(block, c)
        if c > 0:
            value = value + rot[block]
        if c < chunks - 1:
            rot[block] = value
        else:
            sums = lax.dot_general(
                value, weights, (((0,), (0,)), ((), ())), precision=HIGHEST,
                preferred_element_type=jnp.float32,
            )
            for k in range(own_n):
                part[k, block] = sums[k * share:(k + 1) * share]

    load_acts.wait()
    load_own.wait()
    for c in range(chunks):
        add(z, c)

    def step(s):
        for c in range(chunks):
            @pl.when(z - 1 - s >= 0)
            def _():
                from_left(s, c).wait_recv()

                @pl.when(z < n - 1)
                def _():
                    right(s + 1, c).start()

            @pl.when(z + 1 + s < n)
            def _():
                from_right(s, c).wait_recv()

                @pl.when(z > 0)
                def _():
                    left(s + 1, c).start()

            @pl.when(z - 1 - s >= 0)
            def _():
                add(z - 1 - s, c)

            @pl.when(z + 1 + s < n)
            def _():
                add(z + 1 + s, c)

    def settle(s):
        for c in range(chunks):
            @pl.when((z - s >= 0) & (z < n - 1))
            def _():
                right(s, c).wait_send()

            @pl.when((z + s < n) & (z > 0))
            def _():
                left(s, c).wait_send()

    def over_steps(f):
        if n <= 8:
            for s in range(n - 1):
                f(s)
        else:
            lax.fori_loop(0, n - 1, lambda s, carry: (f(s), carry)[1], 0)

    over_steps(step)

    def give(k):
        to = lax.rem(o + k, own_n)
        return pltpu.make_async_remote_copy(
            src_ref=part.at[to], dst_ref=part_in.at[k - 1], send_sem=s1.at[k - 1],
            recv_sem=r1.at[k - 1], device_id={"own": to}, device_id_type=MESH,
        )

    for k in range(1, own_n):
        give(k).start()
    total = part[o]
    for k in range(1, own_n):
        give(k).wait_recv()
        total = total + part_in[k - 1]
    squares = total * total * scale
    folded = squares
    for q in range(1, seqs):
        folded = folded + pltpu.roll(squares, q * half, 2)
    sq[...] = folded

    def give_sq(k):
        to = lax.rem(z + k, n)
        return pltpu.make_async_remote_copy(
            src_ref=sq.at[to], dst_ref=sq_in.at[k - 1], send_sem=s2.at[k - 1],
            recv_sem=r2.at[k - 1], device_id={"blk": to}, device_id_type=MESH,
        )

    if n <= 8:
        for k in range(1, n):
            give_sq(k).start()
        result = sq[z]
        for k in range(1, n):
            give_sq(k).wait_recv()
            result = result + sq_in[k - 1]
        for k in range(1, n):
            give_sq(k).wait_send()
    else:
        def begin(k, carry):
            give_sq(k).start()
            return carry

        def gather(k, value):
            give_sq(k).wait_recv()
            return value + sq_in[k - 1]

        def end(k, carry):
            give_sq(k).wait_send()
            return carry

        lax.fori_loop(1, n, begin, 0)
        result = lax.fori_loop(1, n, gather, sq[z])
        lax.fori_loop(1, n, end, 0)
    out[...] = result
    for k in range(1, own_n):
        give(k).wait_send()
    over_steps(settle)


def per_device(
    activations, rank_grads, lengths, adapter_ids, input_basis, rank_basis, prior_values
):
    n, own_n = lax.axis_size("blk"), lax.axis_size("own")
    tokens, width = activations.shape[1:]
    cols = input_basis.shape[0]
    share = cols // own_n
    seqs = lengths.shape[2]
    adapters, rank = rank_basis.shape[:2]
    lanes = seqs * adapters * rank
    chunks = 4 if n <= 8 else 1
    vmem = pl.BlockSpec(memory_space=pltpu.VMEM)
    smem = pl.BlockSpec(memory_space=pltpu.SMEM)
    anywhere = pl.BlockSpec(memory_space=pl.ANY)
    dma = pltpu.SemaphoreType.DMA
    f32 = jnp.float32
    sums = pl.pallas_call(
        functools.partial(kernel, n, own_n, chunks),
        out_shape=jax.ShapeDtypeStruct((share, lanes), f32),
        in_specs=[smem, smem, anywhere, vmem, anywhere, vmem],
        out_specs=vmem,
        scratch_shapes=[
            pltpu.VMEM((tokens, width), jnp.bfloat16),
            pltpu.VMEM((n, cols, width), jnp.bfloat16),
            pltpu.VMEM((n, tokens, cols), f32),
            pltpu.VMEM((own_n, n, share, lanes), f32),
            pltpu.VMEM((own_n - 1, n, share, lanes), f32),
            pltpu.VMEM((n, share, lanes), f32),
            pltpu.VMEM((n - 1, share, lanes), f32),
            dma((2,)),
            dma((n - 1, chunks)), dma((n - 1, chunks)),
            dma((n - 1, chunks)), dma((n - 1, chunks)),
            dma((own_n - 1,)), dma((own_n - 1,)),
            dma((n - 1,)), dma((n - 1,)),
        ],
        compiler_params=pltpu.CompilerParams(
            collective_id=0, has_side_effects=True, vmem_limit_bytes=48 << 20
        ),
    )(lengths, adapter_ids, activations, rank_grads, input_basis, rank_basis)
    mean_sq = sums[:, :adapters * rank].T.reshape(adapters, rank, share)
    return mean_sq + forget_rate * prior_values


def solution(mesh):
    return jax.shard_map(
        per_device,
        mesh=mesh,
        in_specs=(
            P(None, ("group", "blk"), "own"),
            P(None, ("group", "blk"), None),
            P(None, ("group", "blk"), None),
            P(None, "group"),
            P(("group", "blk"), "own"),
            P("group", None, None),
            P("group", None, ("blk", "own")),
        ),
        out_specs=P("group", None, ("blk", "own")),
        check_vma=False,
    )
```

```python
import functools

import jax
import jax.numpy as jnp
from jax import lax
from jax.experimental import pallas as pl
from jax.experimental.pallas import tpu as pltpu
from jax.sharding import PartitionSpec as P

forget_rate = 0.5
HIGHEST = lax.Precision.HIGHEST
MESH = pl.DeviceIdType.MESH


def kernel(
    n, own_n, chunks,
    lengths_hbm, ids_hbm, acts_hbm, grads_hbm, basis_hbm, rank_basis_hbm, out,
    lengths, ids, grads, rank_basis, acts, panel, rot, part, part_in, sq, sq_in, load_sem, rs, rr, ls, lr, s1, r1, s2, r2,
):
    z = lax.axis_index("blk")
    o = lax.axis_index("own")
    tokens, width = acts.shape
    cols = panel.shape[1]
    share = cols // own_n
    wide = width // chunks
    seqs = lengths.shape[2]
    adapters, rank = rank_basis.shape[0], rank_basis.shape[1]
    lanes = seqs * adapters * rank
    half = adapters * rank

    loads = [
        pltpu.make_async_copy(src, dst, load_sem.at[k])
        for k, (src, dst) in enumerate((
            (lengths_hbm, lengths), (ids_hbm, ids), (grads_hbm, grads),
            (rank_basis_hbm, rank_basis), (basis_hbm, panel.at[z]), (acts_hbm.at[0], acts),
        ))
    ]
    for load in loads:
        load.start()

    barrier = pltpu.get_barrier_semaphore()

    def greet_blk(k, carry):
        pl.semaphore_signal(
            barrier, inc=1, device_id={"blk": lax.rem(z + k, n)}, device_id_type=MESH
        )
        return carry

    lax.fori_loop(1, n, greet_blk, 0)
    for k in range(1, own_n):
        pl.semaphore_signal(
            barrier, inc=1, device_id={"own": lax.rem(o + k, own_n)}, device_id_type=MESH
        )
    pl.semaphore_wait(barrier, n - 1 + own_n - 1)

    def piece(c):
        return pl.ds(c * wide, wide)

    def right(s, c, first=False):
        at = (slice(None), piece(c))
        block = z - s
        return pltpu.make_async_remote_copy(
            src_ref=basis_hbm.at[at] if first else panel.at[(block,) + at],
            dst_ref=panel.at[(block,) + at],
            send_sem=rs.at[s, c], recv_sem=rr.at[s, c],
            device_id={"blk": z + 1}, device_id_type=MESH,
        )

    def left(s, c, first=False):
        at = (slice(None), piece(c))
        block = z + s
        return pltpu.make_async_remote_copy(
            src_ref=basis_hbm.at[at] if first else panel.at[(block,) + at],
            dst_ref=panel.at[(block,) + at],
            send_sem=ls.at[s, c], recv_sem=lr.at[s, c],
            device_id={"blk": z - 1}, device_id_type=MESH,
        )

    def from_left(s, c):
        dst = panel.at[z - 1 - s, :, piece(c)]
        return pltpu.make_async_remote_copy(
            src_ref=dst, dst_ref=dst, send_sem=rs.at[s, c], recv_sem=rr.at[s, c],
            device_id={"blk": z - 1}, device_id_type=MESH,
        )

    def from_right(s, c):
        dst = panel.at[z + 1 + s, :, piece(c)]
        return pltpu.make_async_remote_copy(
            src_ref=dst, dst_ref=dst, send_sem=ls.at[s, c], recv_sem=lr.at[s, c],
            device_id={"blk": z + 1}, device_id_type=MESH,
        )

    for c in range(chunks):
        @pl.when(z < n - 1)
        def _():
            right(0, c, True).start()

        @pl.when(z > 0)
        def _():
            left(0, c, True).start()

    for load in loads[:4]:
        load.wait()

    lane = lax.broadcasted_iota(jnp.int32, (1, lanes), 1)
    lane_seq = lane // half
    lane_adapter = lax.rem(lane // rank, adapters)
    lane_id = jnp.zeros((1, lanes), jnp.int32)
    lane_start = jnp.zeros((1, lanes), jnp.int32)
    lane_end = jnp.zeros((1, lanes), jnp.int32)
    start = jnp.int32(0)
    for q in range(seqs):
        end = start + lengths[0, 0, q]
        here = lane_seq == q
        lane_id = jnp.where(here, ids[0, z * seqs + q], lane_id)
        lane_start = jnp.where(here, start, lane_start)
        lane_end = jnp.where(here, end, lane_end)
        start = end

    def count(k, total):
        return total + jnp.where(lane_adapter == ids[0, k], 1.0, 0.0)

    counts = lax.fori_loop(0, ids.shape[1], count, jnp.zeros((1, lanes), jnp.float32))
    scale = (1.0 - forget_rate) / counts
    spread = jnp.concatenate([rank_basis[a] for a in range(adapters)] * seqs, axis=1)
    spread = jnp.where(lane_id == lane_adapter, spread, 0.0)
    weights = lax.dot_general(
        grads[0].astype(jnp.float32), spread, (((0,), (0,)), ((), ())), precision=HIGHEST,
        preferred_element_type=jnp.float32,
    )
    token = lax.broadcasted_iota(jnp.int32, (tokens, lanes), 0)
    weights = jnp.where((token >= lane_start) & (token < lane_end), weights, 0.0)

    def rotate(block, c):
        return lax.dot_general(
            acts[:, c * wide:(c + 1) * wide], panel[block, :, c * wide:(c + 1) * wide],
            (((1,), (1,)), ((), ())), preferred_element_type=jnp.float32,
        )

    def add(block, c):
        value = rotate(block, c)
        if c > 0:
            value = value + rot[block]
        if c < chunks - 1:
            rot[block] = value
        else:
            sums = lax.dot_general(
                value, weights, (((0,), (0,)), ((), ())), precision=HIGHEST,
                preferred_element_type=jnp.float32,
            )
            for k in range(own_n):
                part[k, block] = sums[k * share:(k + 1) * share]

    for load in loads[4:]:
        load.wait()
    for c in range(chunks):
        add(z, c)

    def step(s):
        for c in range(chunks):
            @pl.when(z - 1 - s >= 0)
            def _():
                from_left(s, c).wait_recv()

                @pl.when(z < n - 1)
                def _():
                    right(s + 1, c).start()

            @pl.when(z + 1 + s < n)
            def _():
                from_right(s, c).wait_recv()

                @pl.when(z > 0)
                def _():
                    left(s + 1, c).start()

            @pl.when(z - 1 - s >= 0)
            def _():
                add(z - 1 - s, c)

            @pl.when(z + 1 + s < n)
            def _():
                add(z + 1 + s, c)

    def settle(s):
        for c in range(chunks):
            @pl.when((z - s >= 0) & (z < n - 1))
            def _():
                right(s, c).wait_send()

            @pl.when((z + s < n) & (z > 0))
            def _():
                left(s, c).wait_send()

    def over_steps(f):
        if n <= 8:
            for s in range(n - 1):
                f(s)
        else:
            lax.fori_loop(0, n - 1, lambda s, carry: (f(s), carry)[1], 0)

    over_steps(step)

    def give(k):
        to = lax.rem(o + k, own_n)
        return pltpu.make_async_remote_copy(
            src_ref=part.at[to], dst_ref=part_in.at[k - 1], send_sem=s1.at[k - 1],
            recv_sem=r1.at[k - 1], device_id={"own": to}, device_id_type=MESH,
        )

    for k in range(1, own_n):
        give(k).start()
    total = part[o]
    for k in range(1, own_n):
        give(k).wait_recv()
        total = total + part_in[k - 1]
    squares = total * total * scale
    folded = squares
    for q in range(1, seqs):
        folded = folded + pltpu.roll(squares, q * half, 2)
    sq[...] = folded

    def give_sq(k):
        to = lax.rem(z + k, n)
        return pltpu.make_async_remote_copy(
            src_ref=sq.at[to], dst_ref=sq_in.at[k - 1], send_sem=s2.at[k - 1],
            recv_sem=r2.at[k - 1], device_id={"blk": to}, device_id_type=MESH,
        )

    if n <= 8:
        for k in range(1, n):
            give_sq(k).start()
        result = sq[z]
        for k in range(1, n):
            give_sq(k).wait_recv()
            result = result + sq_in[k - 1]
        for k in range(1, n):
            give_sq(k).wait_send()
    else:
        def begin(k, carry):
            give_sq(k).start()
            return carry

        def gather(k, value):
            give_sq(k).wait_recv()
            return value + sq_in[k - 1]

        def end(k, carry):
            give_sq(k).wait_send()
            return carry

        lax.fori_loop(1, n, begin, 0)
        result = lax.fori_loop(1, n, gather, sq[z])
        lax.fori_loop(1, n, end, 0)
    for a in range(adapters):
        out[a] = result[:, a * rank:(a + 1) * rank]
    for k in range(1, own_n):
        give(k).wait_send()
    over_steps(settle)


def per_device(
    activations, rank_grads, lengths, adapter_ids, input_basis, rank_basis, prior_values
):
    n, own_n = lax.axis_size("blk"), lax.axis_size("own")
    tokens, width = activations.shape[1:]
    cols = input_basis.shape[0]
    share = cols // own_n
    seqs = lengths.shape[2]
    adapters, rank = rank_basis.shape[:2]
    lanes = seqs * adapters * rank
    chunks = 4 if n <= 8 else 1
    vmem = pl.BlockSpec(memory_space=pltpu.VMEM)
    hbm = pl.BlockSpec(memory_space=pltpu.HBM)
    dma = pltpu.SemaphoreType.DMA
    f32 = jnp.float32
    sums = pl.pallas_call(
        functools.partial(kernel, n, own_n, chunks),
        out_shape=jax.ShapeDtypeStruct((adapters, share, rank), f32),
        in_specs=[hbm] * 6,
        out_specs=vmem,
        scratch_shapes=[
            pltpu.SMEM(lengths.shape, jnp.int32),
            pltpu.SMEM(adapter_ids.shape, jnp.int32),
            pltpu.VMEM((1, rank, tokens), jnp.bfloat16),
            pltpu.VMEM(rank_basis.shape, f32),
            pltpu.VMEM((tokens, width), jnp.bfloat16),
            pltpu.VMEM((n, cols, width), jnp.bfloat16),
            pltpu.VMEM((n, tokens, cols), f32),
            pltpu.VMEM((own_n, n, share, lanes), f32),
            pltpu.VMEM((own_n - 1, n, share, lanes), f32),
            pltpu.VMEM((n, share, lanes), f32),
            pltpu.VMEM((n - 1, share, lanes), f32),
            dma((6,)),
            dma((n - 1, chunks)), dma((n - 1, chunks)),
            dma((n - 1, chunks)), dma((n - 1, chunks)),
            dma((own_n - 1,)), dma((own_n - 1,)),
            dma((n - 1,)), dma((n - 1,)),
        ],
        compiler_params=pltpu.CompilerParams(
            collective_id=0, has_side_effects=True, vmem_limit_bytes=64 << 20
        ),
    )(
        lengths, adapter_ids, activations, jnp.transpose(rank_grads, (0, 2, 1)), input_basis,
        rank_basis,
    )
    prior = jnp.transpose(prior_values, (0, 2, 1))
    return jnp.transpose(sums + forget_rate * prior, (0, 2, 1))


def solution(mesh):
    return jax.shard_map(
        per_device,
        mesh=mesh,
        in_specs=(
            P(None, ("group", "blk"), "own"),
            P(None, ("group", "blk"), None),
            P(None, ("group", "blk"), None),
            P(None, "group"),
            P(("group", "blk"), "own"),
            P("group", None, None),
            P("group", None, ("blk", "own")),
        ),
        out_specs=P("group", None, ("blk", "own")),
        check_vma=False,
    )
```

```python
import functools

import jax
import jax.numpy as jnp
from jax import lax
from jax.experimental import pallas as pl
from jax.experimental.pallas import tpu as pltpu
from jax.sharding import PartitionSpec as P

forget_rate = 0.5
HIGHEST = lax.Precision.HIGHEST
MESH = pl.DeviceIdType.MESH


def kernel(
    n, own_n, chunks,
    lengths_hbm, ids_hbm, acts_hbm, grads_hbm, basis_hbm, rank_basis_hbm, prior_hbm, out,
    lengths, ids, grads, rank_basis, prior, acts, panel, rot, part, part_in, load_sem, rs, rr, ls, lr, send, recv,
):
    z = lax.axis_index("blk")
    o = lax.axis_index("own")
    tokens, width = acts.shape
    cols = panel.shape[1]
    share = cols // own_n
    wide = width // chunks
    seqs = lengths.shape[2]
    adapters, rank = rank_basis.shape[0], rank_basis.shape[1]
    lanes = seqs * adapters * rank
    half = adapters * rank

    loads = [
        pltpu.make_async_copy(src, dst, load_sem.at[k])
        for k, (src, dst) in enumerate((
            (lengths_hbm, lengths), (ids_hbm, ids), (grads_hbm, grads),
            (rank_basis_hbm, rank_basis), (prior_hbm, prior), (basis_hbm, panel.at[z]), (acts_hbm.at[0], acts),
        ))
    ]
    for load in loads:
        load.start()

    barrier = pltpu.get_barrier_semaphore()

    @pl.when(z < n - 1)
    def _():
        pl.semaphore_signal(barrier, inc=1, device_id={"blk": z + 1}, device_id_type=MESH)

    @pl.when(z > 0)
    def _():
        pl.semaphore_signal(barrier, inc=1, device_id={"blk": z - 1}, device_id_type=MESH)

    for k in range(1, own_n):
        pl.semaphore_signal(
            barrier, inc=1, device_id={"own": lax.rem(o + k, own_n)}, device_id_type=MESH
        )
    neighbours = jnp.where(z > 0, 1, 0) + jnp.where(z < n - 1, 1, 0)
    pl.semaphore_wait(barrier, neighbours + own_n - 1)

    def piece(c):
        return pl.ds(c * wide, wide)

    def right(s, c, first=False):
        at = (slice(None), piece(c))
        block = z - s
        return pltpu.make_async_remote_copy(
            src_ref=basis_hbm.at[at] if first else panel.at[(block,) + at],
            dst_ref=panel.at[(block,) + at],
            send_sem=rs.at[s, c], recv_sem=rr.at[s, c],
            device_id={"blk": z + 1}, device_id_type=MESH,
        )

    def left(s, c, first=False):
        at = (slice(None), piece(c))
        block = z + s
        return pltpu.make_async_remote_copy(
            src_ref=basis_hbm.at[at] if first else panel.at[(block,) + at],
            dst_ref=panel.at[(block,) + at],
            send_sem=ls.at[s, c], recv_sem=lr.at[s, c],
            device_id={"blk": z - 1}, device_id_type=MESH,
        )

    def from_left(s, c):
        dst = panel.at[z - 1 - s, :, piece(c)]
        return pltpu.make_async_remote_copy(
            src_ref=dst, dst_ref=dst, send_sem=rs.at[s, c], recv_sem=rr.at[s, c],
            device_id={"blk": z - 1}, device_id_type=MESH,
        )

    def from_right(s, c):
        dst = panel.at[z + 1 + s, :, piece(c)]
        return pltpu.make_async_remote_copy(
            src_ref=dst, dst_ref=dst, send_sem=ls.at[s, c], recv_sem=lr.at[s, c],
            device_id={"blk": z + 1}, device_id_type=MESH,
        )

    for c in range(chunks):
        @pl.when(z < n - 1)
        def _():
            right(0, c, True).start()

        @pl.when(z > 0)
        def _():
            left(0, c, True).start()

    for load in loads[:5]:
        load.wait()

    lane = lax.broadcasted_iota(jnp.int32, (1, lanes), 1)
    lane_seq = lane // half
    lane_adapter = lax.rem(lane // rank, adapters)
    lane_id = jnp.zeros((1, lanes), jnp.int32)
    lane_start = jnp.zeros((1, lanes), jnp.int32)
    lane_end = jnp.zeros((1, lanes), jnp.int32)
    start = jnp.int32(0)
    for q in range(seqs):
        end = start + lengths[0, 0, q]
        here = lane_seq == q
        lane_id = jnp.where(here, ids[0, z * seqs + q], lane_id)
        lane_start = jnp.where(here, start, lane_start)
        lane_end = jnp.where(here, end, lane_end)
        start = end

    def count(k, total):
        return total + jnp.where(lane_adapter == ids[0, k], 1.0, 0.0)

    counts = lax.fori_loop(0, ids.shape[1], count, jnp.zeros((1, lanes), jnp.float32))
    scale = (1.0 - forget_rate) / counts
    spread = jnp.concatenate([rank_basis[a] for a in range(adapters)] * seqs, axis=1)
    spread = jnp.where(lane_id == lane_adapter, spread, 0.0)
    weights = lax.dot_general(
        grads[0].astype(jnp.float32), spread, (((0,), (0,)), ((), ())), precision=HIGHEST,
        preferred_element_type=jnp.float32,
    )
    token = lax.broadcasted_iota(jnp.int32, (tokens, lanes), 0)
    weights = jnp.where((token >= lane_start) & (token < lane_end), weights, 0.0)

    def give(block, k):
        return pltpu.make_async_remote_copy(
            src_ref=part.at[block, k], dst_ref=part_in.at[z, o], send_sem=send.at[block, k],
            recv_sem=recv.at[z, o], device_id={"blk": block, "own": k}, device_id_type=MESH,
        )

    def give_own(k):
        return give(z, lax.rem(o + k, own_n))

    def rotate(block, c):
        return lax.dot_general(
            acts[:, c * wide:(c + 1) * wide], panel[block, :, c * wide:(c + 1) * wide],
            (((1,), (1,)), ((), ())), preferred_element_type=jnp.float32,
        )

    def add(block, c):
        value = rotate(block, c)
        if c > 0:
            value = value + rot[block]
        if c < chunks - 1:
            rot[block] = value
        else:
            sums = lax.dot_general(
                value, weights, (((0,), (0,)), ((), ())), precision=HIGHEST,
                preferred_element_type=jnp.float32,
            )
            for k in range(own_n):
                part[block, k] = sums[k * share:(k + 1) * share]

    for load in loads[5:]:
        load.wait()
    for c in range(chunks):
        add(z, c)
    for k in range(1, own_n):
        give_own(k).start()
    part_in[z, o] = part[z, o]

    def step(s):
        for c in range(chunks):
            @pl.when(z - 1 - s >= 0)
            def _():
                from_left(s, c).wait_recv()

                @pl.when(z < n - 1)
                def _():
                    right(s + 1, c).start()

            @pl.when(z + 1 + s < n)
            def _():
                from_right(s, c).wait_recv()

                @pl.when(z > 0)
                def _():
                    left(s + 1, c).start()

            @pl.when(z - 1 - s >= 0)
            def _():
                add(z - 1 - s, c)
                if c == chunks - 1:
                    for k in range(own_n):
                        give(z - 1 - s, k).start()

            @pl.when(z + 1 + s < n)
            def _():
                add(z + 1 + s, c)
                if c == chunks - 1:
                    for k in range(own_n):
                        give(z + 1 + s, k).start()

    def settle(s):
        for c in range(chunks):
            @pl.when((z - s >= 0) & (z < n - 1))
            def _():
                right(s, c).wait_send()

            @pl.when((z + s < n) & (z > 0))
            def _():
                left(s, c).wait_send()

    def over_steps(f):
        if n <= 8:
            for s in range(n - 1):
                f(s)
        else:
            lax.fori_loop(0, n - 1, lambda s, carry: (f(s), carry)[1], 0)

    over_steps(step)

    def source(zs, k):
        return pltpu.make_async_remote_copy(
            src_ref=part_in.at[zs, k], dst_ref=part_in.at[zs, k], send_sem=send.at[zs, k],
            recv_sem=recv.at[zs, k], device_id={"blk": zs, "own": k}, device_id_type=MESH,
        )

    for k in range(1, own_n):
        source(z, lax.rem(o + k, own_n)).wait_recv()

    def squares(zs):
        total = part_in[zs, 0]
        for k in range(1, own_n):
            total = total + part_in[zs, k]
        return total * total

    def gather(k, value):
        zs = lax.rem(z + k, n)
        for q in range(own_n):
            source(zs, q).wait_recv()
        return value + squares(zs)

    def settle_sums(k, carry):
        for q in range(own_n):
            give(lax.rem(z + k, n), q).wait_send()
        return carry

    result = squares(z)
    if n <= 8:
        for k in range(1, n):
            result = gather(k, result)
    else:
        result = lax.fori_loop(1, n, gather, result)
    result = result * scale
    folded = result
    for q in range(1, seqs):
        folded = folded + pltpu.roll(result, q * half, 1)
    result = folded
    for a in range(adapters):
        out[a] = result[:, a * rank:(a + 1) * rank] + forget_rate * prior[a]
    for k in range(1, own_n):
        give_own(k).wait_send()
    lax.fori_loop(1, n, settle_sums, 0)
    over_steps(settle)


def per_device(
    activations, rank_grads, lengths, adapter_ids, input_basis, rank_basis, prior_values
):
    n, own_n = lax.axis_size("blk"), lax.axis_size("own")
    tokens, width = activations.shape[1:]
    cols = input_basis.shape[0]
    share = cols // own_n
    seqs = lengths.shape[2]
    adapters, rank = rank_basis.shape[:2]
    lanes = seqs * adapters * rank
    chunks = 4 if n <= 8 else 1
    vmem = pl.BlockSpec(memory_space=pltpu.VMEM)
    hbm = pl.BlockSpec(memory_space=pltpu.HBM)
    dma = pltpu.SemaphoreType.DMA
    f32 = jnp.float32
    sums = pl.pallas_call(
        functools.partial(kernel, n, own_n, chunks),
        out_shape=jax.ShapeDtypeStruct((adapters, share, rank), f32),
        in_specs=[hbm] * 7,
        out_specs=vmem,
        scratch_shapes=[
            pltpu.SMEM(lengths.shape, jnp.int32),
            pltpu.SMEM(adapter_ids.shape, jnp.int32),
            pltpu.VMEM((1, rank, tokens), jnp.bfloat16),
            pltpu.VMEM(rank_basis.shape, f32),
            pltpu.VMEM((adapters, share, rank), f32),
            pltpu.VMEM((tokens, width), jnp.bfloat16),
            pltpu.VMEM((n, cols, width), jnp.bfloat16),
            pltpu.VMEM((n, tokens, cols), f32),
            pltpu.VMEM((n, own_n, share, lanes), f32),
            pltpu.VMEM((n, own_n, share, lanes), f32),
            dma((7,)),
            dma((n - 1, chunks)), dma((n - 1, chunks)),
            dma((n - 1, chunks)), dma((n - 1, chunks)),
            dma((n, own_n)), dma((n, own_n)),
        ],
        compiler_params=pltpu.CompilerParams(
            collective_id=0, has_side_effects=True, vmem_limit_bytes=64 << 20
        ),
    )(
        lengths, adapter_ids, activations, jnp.transpose(rank_grads, (0, 2, 1)), input_basis,
        rank_basis, jnp.transpose(prior_values, (0, 2, 1)),
    )
    return jnp.transpose(sums, (0, 2, 1))


def solution(mesh):
    return jax.shard_map(
        per_device,
        mesh=mesh,
        in_specs=(
            P(None, ("group", "blk"), "own"),
            P(None, ("group", "blk"), None),
            P(None, ("group", "blk"), None),
            P(None, "group"),
            P(("group", "blk"), "own"),
            P("group", None, None),
            P("group", None, ("blk", "own")),
        ),
        out_specs=P("group", None, ("blk", "own")),
        check_vma=False,
    )
```

```python
import functools

import jax
import jax.numpy as jnp
from jax import lax
from jax.experimental import pallas as pl
from jax.experimental.pallas import tpu as pltpu
from jax.sharding import PartitionSpec as P

forget_rate = 0.5
HIGHEST = lax.Precision.HIGHEST
MESH = pl.DeviceIdType.MESH


def kernel(
    n, own_n, pieces, helped,
    lengths_hbm, ids_hbm, acts_hbm, grads_hbm, basis_hbm, rank_basis_hbm, prior_hbm, out,
    lengths, ids, grads, rank_basis, prior, acts, panel, rot, part, part_in, load_sem, rs, rr, ls, lr, send, recv,
    up, up_in, aid, aid_in, up_sem, aid_send, aid_recv,
):
    z = lax.axis_index("blk")
    o = lax.axis_index("own")
    tokens, width = acts.shape
    cols = panel.shape[1]
    share = cols // own_n
    chunks = len(pieces)
    bf16, f32 = jnp.bfloat16, jnp.float32
    seqs = lengths.shape[2]
    adapters, rank = rank_basis.shape[0], rank_basis.shape[1]
    lanes = seqs * adapters * rank
    half = adapters * rank

    loads = [
        pltpu.make_async_copy(src, dst, load_sem.at[k])
        for k, (src, dst) in enumerate((
            (lengths_hbm, lengths), (ids_hbm, ids), (grads_hbm, grads),
            (rank_basis_hbm, rank_basis), (prior_hbm, prior), (basis_hbm, panel.at[z]), (acts_hbm.at[0], acts),
        ))
    ]
    for load in loads:
        load.start()

    barrier = pltpu.get_barrier_semaphore()

    @pl.when(z < n - 1)
    def _():
        pl.semaphore_signal(barrier, inc=1, device_id={"blk": z + 1}, device_id_type=MESH)

    @pl.when(z > 0)
    def _():
        pl.semaphore_signal(barrier, inc=1, device_id={"blk": z - 1}, device_id_type=MESH)

    for k in range(1, own_n):
        pl.semaphore_signal(
            barrier, inc=1, device_id={"own": lax.rem(o + k, own_n)}, device_id_type=MESH
        )
    neighbours = jnp.where(z > 0, 1, 0) + jnp.where(z < n - 1, 1, 0)
    pl.semaphore_wait(barrier, neighbours + own_n - 1)

    def piece(c):
        return pl.ds(*pieces[c])

    def goes_right(c):
        return z < (n - 2 if helped and c == 0 else n - 1)

    def goes_left(c):
        return z > (1 if helped and c == 0 else 0)

    def comes_left(s, c):
        there = z - 1 - s >= 0
        return there & (z < n - 1) if helped and c == 0 else there

    def comes_right(s, c):
        there = z + 1 + s < n
        return there & (z > 0) if helped and c == 0 else there

    def right(s, c, first=False):
        at = (slice(None), piece(c))
        block = z - s
        return pltpu.make_async_remote_copy(
            src_ref=basis_hbm.at[at] if first else panel.at[(block,) + at],
            dst_ref=panel.at[(block,) + at],
            send_sem=rs.at[s, c], recv_sem=rr.at[s, c],
            device_id={"blk": z + 1}, device_id_type=MESH,
        )

    def left(s, c, first=False):
        at = (slice(None), piece(c))
        block = z + s
        return pltpu.make_async_remote_copy(
            src_ref=basis_hbm.at[at] if first else panel.at[(block,) + at],
            dst_ref=panel.at[(block,) + at],
            send_sem=ls.at[s, c], recv_sem=lr.at[s, c],
            device_id={"blk": z - 1}, device_id_type=MESH,
        )

    def from_left(s, c):
        dst = panel.at[z - 1 - s, :, piece(c)]
        return pltpu.make_async_remote_copy(
            src_ref=dst, dst_ref=dst, send_sem=rs.at[s, c], recv_sem=rr.at[s, c],
            device_id={"blk": z - 1}, device_id_type=MESH,
        )

    def from_right(s, c):
        dst = panel.at[z + 1 + s, :, piece(c)]
        return pltpu.make_async_remote_copy(
            src_ref=dst, dst_ref=dst, send_sem=ls.at[s, c], recv_sem=lr.at[s, c],
            device_id={"blk": z + 1}, device_id_type=MESH,
        )

    for c in range(chunks):
        @pl.when(goes_right(c))
        def _():
            right(0, c, True).start()

        @pl.when(goes_left(c))
        def _():
            left(0, c, True).start()

    for load in loads[:5]:
        load.wait()

    lane = lax.broadcasted_iota(jnp.int32, (1, lanes), 1)
    lane_seq = lane // half
    lane_adapter = lax.rem(lane // rank, adapters)
    lane_id = jnp.zeros((1, lanes), jnp.int32)
    lane_start = jnp.zeros((1, lanes), jnp.int32)
    lane_end = jnp.zeros((1, lanes), jnp.int32)
    start = jnp.int32(0)
    for q in range(seqs):
        end = start + lengths[0, 0, q]
        here = lane_seq == q
        lane_id = jnp.where(here, ids[0, z * seqs + q], lane_id)
        lane_start = jnp.where(here, start, lane_start)
        lane_end = jnp.where(here, end, lane_end)
        start = end

    def count(k, total):
        return total + jnp.where(lane_adapter == ids[0, k], 1.0, 0.0)

    counts = lax.fori_loop(0, ids.shape[1], count, jnp.zeros((1, lanes), jnp.float32))
    scale = (1.0 - forget_rate) / counts
    spread = jnp.concatenate([rank_basis[a] for a in range(adapters)] * seqs, axis=1)
    spread = jnp.where(lane_id == lane_adapter, spread, 0.0)
    weights = lax.dot_general(
        grads[0].astype(jnp.float32), spread, (((0,), (0,)), ((), ())), precision=HIGHEST,
        preferred_element_type=jnp.float32,
    )
    token = lax.broadcasted_iota(jnp.int32, (tokens, lanes), 0)
    weights = jnp.where((token >= lane_start) & (token < lane_end), weights, 0.0)

    def give(block, k):
        return pltpu.make_async_remote_copy(
            src_ref=part.at[block, k], dst_ref=part_in.at[z, o], send_sem=send.at[block, k],
            recv_sem=recv.at[z, o], device_id={"blk": block, "own": k}, device_id_type=MESH,
        )

    def give_own(k):
        return give(z, lax.rem(o + k, own_n))

    def rotate(block, c):
        return lax.dot_general(
            acts[:, piece(c)], panel[block, :, piece(c)],
            (((1,), (1,)), ((), ())), preferred_element_type=jnp.float32,
        )

    def add(block, c):
        value = rotate(block, c) + rot[block]
        if c < chunks - 1:
            rot[block] = value
        else:
            sums = lax.dot_general(
                value, weights, (((0,), (0,)), ((), ())), precision=HIGHEST,
                preferred_element_type=jnp.float32,
            )
            for k in range(own_n):
                part[block, k] = sums[k * share:(k + 1) * share]

    for load in loads[5:]:
        load.wait()
    rot[...] = jnp.zeros_like(rot)
    end = jnp.where(z < n // 2, 0, n - 1)
    side = jnp.where(z < n // 2, 0, 1)
    is_end = (z == 0) | (z == n - 1)
    is_aid = (z == 1) | (z == n - 2)
    other = jnp.where(z < n // 2, 1 - z, 2 * n - 3 - z)

    def send_up():
        return pltpu.make_async_remote_copy(
            src_ref=up, dst_ref=up_in, send_sem=up_sem.at[0], recv_sem=up_sem.at[1],
            device_id={"blk": other}, device_id_type=MESH,
        )

    if helped:
        @pl.when(is_end)
        def _():
            rows = jnp.concatenate(
                [
                    sum(
                        weights[:, (q * adapters + a) * rank:(q * adapters + a + 1) * rank]
                        for a in range(adapters)
                    )
                    for q in range(seqs)
                ],
                axis=1,
            )
            terms, rest = [], rows
            for _ in range(3):
                term = rest.astype(bf16)
                terms.append(lax.dot_general(
                    term, acts[:, piece(0)], (((0,), (0,)), ((), ())),
                    preferred_element_type=f32,
                ))
                rest = rest - term.astype(f32)
            grouped = terms[2] + terms[1] + terms[0]
            high = grouped.astype(bf16)
            up[:seqs * rank] = high
            up[seqs * rank:] = (grouped - high.astype(f32)).astype(bf16)
            send_up().start()

    def give_aid(block, k):
        return pltpu.make_async_remote_copy(
            src_ref=aid.at[block, k], dst_ref=aid_in.at[side, o], send_sem=aid_send.at[block, k],
            recv_sem=aid_recv.at[side, o], device_id={"blk": block, "own": k},
            device_id_type=MESH,
        )

    def aid_block(k):
        return jnp.where(end == 0, n - k, k - 1)

    def help_end():
        send_up().wait_recv()
        for k in range(1, n):
            block = aid_block(k)
            both = lax.dot_general(
                panel[block, :, piece(0)], up_in[...], (((1,), (1,)), ((), ())),
                preferred_element_type=f32,
            )
            sums = both[:, :seqs * rank] + both[:, seqs * rank:]
            sums = jnp.concatenate(
                [
                    sums[:, q * rank:(q + 1) * rank]
                    for q in range(seqs) for _ in range(adapters)
                ],
                axis=1,
            )
            end_id = jnp.zeros((1, lanes), jnp.int32)
            for q in range(seqs):
                end_id = jnp.where(lane_seq == q, ids[0, end * seqs + q], end_id)
            sums = jnp.where(end_id == lane_adapter, sums, 0.0)
            for j in range(own_n):
                aid[block, j] = sums[j * share:(j + 1) * share]
            for j in range(own_n):
                @pl.when((block != z) | (o != j))
                def _():
                    give_aid(block, j).start()

            @pl.when(block == z)
            def _():
                aid_in[side, o] = aid[z, o]

    def settle_aid():
        for k in range(1, n):
            block = aid_block(k)
            for j in range(own_n):
                @pl.when((block != z) | (o != j))
                def _():
                    give_aid(block, j).wait_send()

    def from_aid(which, k):
        return pltpu.make_async_remote_copy(
            src_ref=aid_in.at[which, k], dst_ref=aid_in.at[which, k],
            send_sem=aid_recv.at[which, k], recv_sem=aid_recv.at[which, k],
            device_id={"blk": other, "own": k}, device_id_type=MESH,
        )

    for c in range(chunks):
        add(z, c)
    for k in range(1, own_n):
        give_own(k).start()
    part_in[z, o] = part[z, o]

    def step(s):
        for c in range(chunks):
            @pl.when(comes_left(s, c))
            def _():
                from_left(s, c).wait_recv()

                @pl.when(goes_right(c))
                def _():
                    right(s + 1, c).start()

            @pl.when(comes_right(s, c))
            def _():
                from_right(s, c).wait_recv()

                @pl.when(goes_left(c))
                def _():
                    left(s + 1, c).start()

            @pl.when(comes_left(s, c))
            def _():
                add(z - 1 - s, c)
                if c == chunks - 1:
                    for k in range(own_n):
                        give(z - 1 - s, k).start()

            @pl.when(comes_right(s, c))
            def _():
                add(z + 1 + s, c)
                if c == chunks - 1:
                    for k in range(own_n):
                        give(z + 1 + s, k).start()

    def settle(s):
        for c in range(chunks):
            @pl.when((z - s >= 0) & goes_right(c))
            def _():
                right(s, c).wait_send()

            @pl.when((z + s < n) & goes_left(c))
            def _():
                left(s, c).wait_send()

    def over_steps(f):
        if n <= 8:
            for s in range(n - 1):
                f(s)
        else:
            lax.fori_loop(0, n - 1, lambda s, carry: (f(s), carry)[1], 0)

    over_steps(step)
    if helped:
        pl.when(is_aid)(help_end)

    def source(zs, k):
        return pltpu.make_async_remote_copy(
            src_ref=part_in.at[zs, k], dst_ref=part_in.at[zs, k], send_sem=send.at[zs, k],
            recv_sem=recv.at[zs, k], device_id={"blk": zs, "own": k}, device_id_type=MESH,
        )

    for k in range(1, own_n):
        source(z, lax.rem(o + k, own_n)).wait_recv()

    def squares(zs):
        total = part_in[zs, 0]
        for k in range(1, own_n):
            total = total + part_in[zs, k]
        if helped:
            more = aid_in[jnp.where(zs == 0, 0, 1), 0]
            for k in range(1, own_n):
                more = more + aid_in[jnp.where(zs == 0, 0, 1), k]
            helps = jnp.where(((zs == 0) | (zs == n - 1)) & (zs != z), 1, 0)
            total = total + jnp.where(jnp.full(total.shape, helps) == 1, more, 0.0)
        return total * total

    def gather(k, value):
        zs = lax.rem(z + k, n)
        for q in range(own_n):
            source(zs, q).wait_recv()
        return value + squares(zs)

    def settle_sums(k, carry):
        for q in range(own_n):
            give(lax.rem(z + k, n), q).wait_send()
        return carry

    if n <= 8:
        for k in range(1, n):
            for q in range(own_n):
                source(lax.rem(z + k, n), q).wait_recv()
        if helped:
            for which in range(2):
                for q in range(own_n):
                    mine = (z == (1, n - 2)[which]) & (o == q)

                    @pl.when((z != (0, n - 1)[which]) & jnp.logical_not(mine))
                    def _():
                        from_aid(which, q).wait_recv()
        result = squares(z)
        for k in range(1, n):
            result = result + squares(lax.rem(z + k, n))
    else:
        result = lax.fori_loop(1, n, gather, squares(z))
    result = result * scale
    folded = result
    for q in range(1, seqs):
        folded = folded + pltpu.roll(result, q * half, 1)
    result = folded
    for a in range(adapters):
        out[a] = result[:, a * rank:(a + 1) * rank] + forget_rate * prior[a]
    for k in range(1, own_n):
        give_own(k).wait_send()
    lax.fori_loop(1, n, settle_sums, 0)
    if helped:
        @pl.when(is_end)
        def _():
            send_up().wait_send()

        pl.when(is_aid)(settle_aid)
    over_steps(settle)


def cut(width, n, helped):
    if n > 8:
        return ((0, width),)
    tiles = width // 128
    first = max(1, tiles * 2 // 7) if helped else 0
    count = 4
    edges = [first + (tiles - first) * k // count for k in range(count + 1)]
    if helped:
        edges = [0] + edges
    return tuple((int(a * 128), int((b - a) * 128)) for a, b in zip(edges, edges[1:]))


def per_device(
    activations, rank_grads, lengths, adapter_ids, input_basis, rank_basis, prior_values
):
    n, own_n = lax.axis_size("blk"), lax.axis_size("own")
    tokens, width = activations.shape[1:]
    cols = input_basis.shape[0]
    share = cols // own_n
    seqs = lengths.shape[2]
    adapters, rank = rank_basis.shape[:2]
    lanes = seqs * adapters * rank
    helped = 4 <= n <= 8
    pieces = cut(width, n, helped)
    chunks = len(pieces)
    first = pieces[0][1] if helped else 128
    terms = 2 * seqs * rank
    vmem = pl.BlockSpec(memory_space=pltpu.VMEM)
    hbm = pl.BlockSpec(memory_space=pltpu.HBM)
    dma = pltpu.SemaphoreType.DMA
    f32 = jnp.float32
    sums = pl.pallas_call(
        functools.partial(kernel, n, own_n, pieces, helped),
        out_shape=jax.ShapeDtypeStruct((adapters, share, rank), f32),
        in_specs=[hbm] * 7,
        out_specs=vmem,
        scratch_shapes=[
            pltpu.SMEM(lengths.shape, jnp.int32),
            pltpu.SMEM(adapter_ids.shape, jnp.int32),
            pltpu.VMEM((1, rank, tokens), jnp.bfloat16),
            pltpu.VMEM(rank_basis.shape, f32),
            pltpu.VMEM((adapters, share, rank), f32),
            pltpu.VMEM((tokens, width), jnp.bfloat16),
            pltpu.VMEM((n, cols, width), jnp.bfloat16),
            pltpu.VMEM((n, tokens, cols), f32),
            pltpu.VMEM((n, own_n, share, lanes), f32),
            pltpu.VMEM((n, own_n, share, lanes), f32),
            dma((7,)),
            dma((n - 1, chunks)), dma((n - 1, chunks)),
            dma((n - 1, chunks)), dma((n - 1, chunks)),
            dma((n, own_n)), dma((n, own_n)),
            pltpu.VMEM((terms, first), jnp.bfloat16),
            pltpu.VMEM((terms, first), jnp.bfloat16),
            pltpu.VMEM((n if helped else 1, own_n, share, lanes), f32),
            pltpu.VMEM((2, own_n, share, lanes), f32),
            dma((2,)), dma((n, own_n)), dma((2, own_n)),
        ],
        compiler_params=pltpu.CompilerParams(
            collective_id=0, has_side_effects=True, vmem_limit_bytes=64 << 20
        ),
    )(
        lengths, adapter_ids, activations, jnp.transpose(rank_grads, (0, 2, 1)), input_basis,
        rank_basis, jnp.transpose(prior_values, (0, 2, 1)),
    )
    return jnp.transpose(sums, (0, 2, 1))


def solution(mesh):
    return jax.shard_map(
        per_device,
        mesh=mesh,
        in_specs=(
            P(None, ("group", "blk"), "own"),
            P(None, ("group", "blk"), None),
            P(None, ("group", "blk"), None),
            P(None, "group"),
            P(("group", "blk"), "own"),
            P("group", None, None),
            P("group", None, ("blk", "own")),
        ),
        out_specs=P("group", None, ("blk", "own")),
        check_vma=False,
    )
```

```python
import functools

import jax
import jax.numpy as jnp
from jax import lax
from jax.experimental import pallas as pl
from jax.experimental.pallas import tpu as pltpu
from jax.sharding import PartitionSpec as P

forget_rate = 0.5
HIGHEST = lax.Precision.HIGHEST
MESH = pl.DeviceIdType.MESH


def kernel(
    n, own_n, pieces, helped,
    lengths_hbm, ids_hbm, acts_hbm, grads_hbm, basis_hbm, rank_basis_hbm, prior_hbm, out,
    lengths, ids, grads, rank_basis, prior, acts, panel, rot, part, part_in, load_sem, rs, rr, ls, lr, send, recv,
    up, up_in, aid, aid_in, up_sem, aid_send, aid_recv,
):
    z = lax.axis_index("blk")
    o = lax.axis_index("own")
    tokens, width = acts.shape
    cols = panel.shape[1]
    share = cols // own_n
    chunks = len(pieces)
    bf16, f32 = jnp.bfloat16, jnp.float32
    seqs = lengths.shape[2]
    adapters, rank = rank_basis.shape[0], rank_basis.shape[1]
    lanes = seqs * adapters * rank
    half = adapters * rank

    loads = [
        pltpu.make_async_copy(src, dst, load_sem.at[k])
        for k, (src, dst) in enumerate((
            (lengths_hbm, lengths), (ids_hbm, ids), (grads_hbm, grads),
            (rank_basis_hbm, rank_basis), (prior_hbm, prior), (basis_hbm, panel.at[z]), (acts_hbm.at[0], acts),
        ))
    ]

    barrier = pltpu.get_barrier_semaphore()

    @pl.when(z < n - 1)
    def _():
        pl.semaphore_signal(barrier, inc=1, device_id={"blk": z + 1}, device_id_type=MESH)

    @pl.when(z > 0)
    def _():
        pl.semaphore_signal(barrier, inc=1, device_id={"blk": z - 1}, device_id_type=MESH)

    for k in range(1, own_n):
        pl.semaphore_signal(
            barrier, inc=1, device_id={"own": lax.rem(o + k, own_n)}, device_id_type=MESH
        )
    for load in loads:
        load.start()
    neighbours = jnp.where(z > 0, 1, 0) + jnp.where(z < n - 1, 1, 0)
    pl.semaphore_wait(barrier, neighbours + own_n - 1)

    def piece(c):
        return pl.ds(*pieces[c])

    def goes_right(c):
        return z < (n - 2 if helped and c == 0 else n - 1)

    def goes_left(c):
        return z > (1 if helped and c == 0 else 0)

    def comes_left(s, c):
        there = z - 1 - s >= 0
        return there & (z < n - 1) if helped and c == 0 else there

    def comes_right(s, c):
        there = z + 1 + s < n
        return there & (z > 0) if helped and c == 0 else there

    def right(s, c, first=False):
        at = (slice(None), piece(c))
        block = z - s
        return pltpu.make_async_remote_copy(
            src_ref=basis_hbm.at[at] if first else panel.at[(block,) + at],
            dst_ref=panel.at[(block,) + at],
            send_sem=rs.at[s, c], recv_sem=rr.at[s, c],
            device_id={"blk": z + 1}, device_id_type=MESH,
        )

    def left(s, c, first=False):
        at = (slice(None), piece(c))
        block = z + s
        return pltpu.make_async_remote_copy(
            src_ref=basis_hbm.at[at] if first else panel.at[(block,) + at],
            dst_ref=panel.at[(block,) + at],
            send_sem=ls.at[s, c], recv_sem=lr.at[s, c],
            device_id={"blk": z - 1}, device_id_type=MESH,
        )

    def from_left(s, c):
        dst = panel.at[z - 1 - s, :, piece(c)]
        return pltpu.make_async_remote_copy(
            src_ref=dst, dst_ref=dst, send_sem=rs.at[s, c], recv_sem=rr.at[s, c],
            device_id={"blk": z - 1}, device_id_type=MESH,
        )

    def from_right(s, c):
        dst = panel.at[z + 1 + s, :, piece(c)]
        return pltpu.make_async_remote_copy(
            src_ref=dst, dst_ref=dst, send_sem=ls.at[s, c], recv_sem=lr.at[s, c],
            device_id={"blk": z + 1}, device_id_type=MESH,
        )

    for c in range(chunks):
        @pl.when(goes_right(c))
        def _():
            right(0, c, True).start()

        @pl.when(goes_left(c))
        def _():
            left(0, c, True).start()

    for load in loads[:5]:
        load.wait()

    lane = lax.broadcasted_iota(jnp.int32, (1, lanes), 1)
    lane_seq = lane // half
    lane_adapter = lax.rem(lane // rank, adapters)
    lane_id = jnp.zeros((1, lanes), jnp.int32)
    lane_start = jnp.zeros((1, lanes), jnp.int32)
    lane_end = jnp.zeros((1, lanes), jnp.int32)
    start = jnp.int32(0)
    for q in range(seqs):
        end = start + lengths[0, 0, q]
        here = lane_seq == q
        lane_id = jnp.where(here, ids[0, z * seqs + q], lane_id)
        lane_start = jnp.where(here, start, lane_start)
        lane_end = jnp.where(here, end, lane_end)
        start = end

    def count(k, total):
        return total + jnp.where(lane_adapter == ids[0, k], 1.0, 0.0)

    counts = lax.fori_loop(0, ids.shape[1], count, jnp.zeros((1, lanes), jnp.float32))
    scale = (1.0 - forget_rate) / counts
    spread = jnp.concatenate([rank_basis[a] for a in range(adapters)] * seqs, axis=1)
    spread = jnp.where(lane_id == lane_adapter, spread, 0.0)
    weights = lax.dot_general(
        grads[0].astype(jnp.float32), spread, (((0,), (0,)), ((), ())), precision=HIGHEST,
        preferred_element_type=jnp.float32,
    )
    token = lax.broadcasted_iota(jnp.int32, (tokens, lanes), 0)
    weights = jnp.where((token >= lane_start) & (token < lane_end), weights, 0.0)

    def give(block, k):
        return pltpu.make_async_remote_copy(
            src_ref=part.at[block, k], dst_ref=part_in.at[z, o], send_sem=send.at[block, k],
            recv_sem=recv.at[z, o], device_id={"blk": block, "own": k}, device_id_type=MESH,
        )

    def give_own(k):
        return give(z, lax.rem(o + k, own_n))

    def rotate(block, c):
        return lax.dot_general(
            panel[block, :, piece(c)], acts[:, piece(c)],
            (((1,), (1,)), ((), ())), preferred_element_type=jnp.float32,
        )

    def add(block, c):
        value = rotate(block, c) + rot[block]
        if c < chunks - 1:
            rot[block] = value
        else:
            sums = lax.dot_general(
                value, weights, (((1,), (0,)), ((), ())), precision=HIGHEST,
                preferred_element_type=jnp.float32,
            )
            for k in range(own_n):
                part[block, k] = sums[k * share:(k + 1) * share]

    for load in loads[5:]:
        load.wait()
    rot[...] = jnp.zeros_like(rot)
    end = jnp.where(z < n // 2, 0, n - 1)
    side = jnp.where(z < n // 2, 0, 1)
    is_end = (z == 0) | (z == n - 1)
    is_aid = (z == 1) | (z == n - 2)
    other = jnp.where(z < n // 2, 1 - z, 2 * n - 3 - z)

    def send_up():
        return pltpu.make_async_remote_copy(
            src_ref=up, dst_ref=up_in, send_sem=up_sem.at[0], recv_sem=up_sem.at[1],
            device_id={"blk": other}, device_id_type=MESH,
        )

    if helped:
        @pl.when(is_end)
        def _():
            rows = jnp.concatenate(
                [
                    sum(
                        weights[:, (q * adapters + a) * rank:(q * adapters + a + 1) * rank]
                        for a in range(adapters)
                    )
                    for q in range(seqs)
                ],
                axis=1,
            )
            terms, rest = [], rows
            for _ in range(3):
                term = rest.astype(bf16)
                terms.append(lax.dot_general(
                    term, acts[:, piece(0)], (((0,), (0,)), ((), ())),
                    preferred_element_type=f32,
                ))
                rest = rest - term.astype(f32)
            grouped = terms[2] + terms[1] + terms[0]
            high = grouped.astype(bf16)
            up[:seqs * rank] = high
            up[seqs * rank:] = (grouped - high.astype(f32)).astype(bf16)
            send_up().start()

    def give_aid(block, k):
        return pltpu.make_async_remote_copy(
            src_ref=aid.at[block, k], dst_ref=aid_in.at[side, o], send_sem=aid_send.at[block, k],
            recv_sem=aid_recv.at[side, o], device_id={"blk": block, "own": k},
            device_id_type=MESH,
        )

    def aid_block(k):
        return jnp.where(end == 0, n - k, k - 1)

    def help_end():
        send_up().wait_recv()
        rows = n * cols
        both = lax.dot_general(
            panel[:, :, piece(0)].reshape(rows, pieces[0][1]), up_in[...],
            (((1,), (1,)), ((), ())), preferred_element_type=f32,
        )
        sums = both[:, :seqs * rank] + both[:, seqs * rank:]
        sums = jnp.concatenate(
            [
                sums[:, q * rank:(q + 1) * rank]
                for q in range(seqs) for _ in range(adapters)
            ],
            axis=1,
        )
        end_id = jnp.zeros((1, lanes), jnp.int32)
        for q in range(seqs):
            end_id = jnp.where(lane_seq == q, ids[0, end * seqs + q], end_id)
        sums = jnp.where(end_id == lane_adapter, sums, 0.0)
        for k in range(n):
            for j in range(own_n):
                at = k * cols + j * share
                aid[k, j] = sums[at:at + share]
        for k in range(1, n):
            block = aid_block(k)
            for j in range(own_n):
                @pl.when((block != z) | (o != j))
                def _():
                    give_aid(block, j).start()

        aid_in[side, o] = aid[z, o]

    def settle_aid():
        for k in range(1, n):
            block = aid_block(k)
            for j in range(own_n):
                @pl.when((block != z) | (o != j))
                def _():
                    give_aid(block, j).wait_send()

    def from_aid(which, k):
        return pltpu.make_async_remote_copy(
            src_ref=aid_in.at[which, k], dst_ref=aid_in.at[which, k],
            send_sem=aid_recv.at[which, k], recv_sem=aid_recv.at[which, k],
            device_id={"blk": other, "own": k}, device_id_type=MESH,
        )

    for c in range(chunks):
        add(z, c)
    for k in range(1, own_n):
        give_own(k).start()
    part_in[z, o] = part[z, o]

    def step(s):
        for c in range(chunks):
            @pl.when(comes_left(s, c))
            def _():
                from_left(s, c).wait_recv()

                @pl.when(goes_right(c))
                def _():
                    right(s + 1, c).start()

            @pl.when(comes_right(s, c))
            def _():
                from_right(s, c).wait_recv()

                @pl.when(goes_left(c))
                def _():
                    left(s + 1, c).start()

            @pl.when(comes_left(s, c))
            def _():
                add(z - 1 - s, c)
                if c == chunks - 1:
                    for k in range(own_n):
                        give(z - 1 - s, k).start()

            @pl.when(comes_right(s, c))
            def _():
                add(z + 1 + s, c)
                if c == chunks - 1:
                    for k in range(own_n):
                        give(z + 1 + s, k).start()

    def settle(s):
        for c in range(chunks):
            @pl.when((z - s >= 0) & goes_right(c))
            def _():
                right(s, c).wait_send()

            @pl.when((z + s < n) & goes_left(c))
            def _():
                left(s, c).wait_send()

    def over_steps(f):
        if n <= 8:
            for s in range(n - 1):
                f(s)
        else:
            lax.fori_loop(0, n - 1, lambda s, carry: (f(s), carry)[1], 0)

    over_steps(step)
    if helped:
        pl.when(is_aid)(help_end)

    def source(zs, k):
        return pltpu.make_async_remote_copy(
            src_ref=part_in.at[zs, k], dst_ref=part_in.at[zs, k], send_sem=send.at[zs, k],
            recv_sem=recv.at[zs, k], device_id={"blk": zs, "own": k}, device_id_type=MESH,
        )

    for k in range(1, own_n):
        source(z, lax.rem(o + k, own_n)).wait_recv()

    def squares(zs):
        total = part_in[zs, 0]
        for k in range(1, own_n):
            total = total + part_in[zs, k]
        if helped:
            more = aid_in[jnp.where(zs == 0, 0, 1), 0]
            for k in range(1, own_n):
                more = more + aid_in[jnp.where(zs == 0, 0, 1), k]
            helps = jnp.where(((zs == 0) | (zs == n - 1)) & (zs != z), 1, 0)
            total = total + jnp.where(jnp.full(total.shape, helps) == 1, more, 0.0)
        return total * total

    def gather(k, value):
        zs = lax.rem(z + k, n)
        for q in range(own_n):
            source(zs, q).wait_recv()
        return value + squares(zs)

    def settle_sums(k, carry):
        for q in range(own_n):
            give(lax.rem(z + k, n), q).wait_send()
        return carry

    if n <= 8:
        for k in range(1, n):
            for q in range(own_n):
                source(lax.rem(z + k, n), q).wait_recv()
        if helped:
            for which in range(2):
                for q in range(own_n):
                    mine = (z == (1, n - 2)[which]) & (o == q)

                    @pl.when((z != (0, n - 1)[which]) & jnp.logical_not(mine))
                    def _():
                        from_aid(which, q).wait_recv()
        result = squares(z)
        for k in range(1, n):
            result = result + squares(lax.rem(z + k, n))
    else:
        result = lax.fori_loop(1, n, gather, squares(z))
    result = result * scale
    folded = result
    for q in range(1, seqs):
        folded = folded + pltpu.roll(result, q * half, 1)
    result = folded
    for a in range(adapters):
        out[a] = result[:, a * rank:(a + 1) * rank] + forget_rate * prior[a]
    for k in range(1, own_n):
        give_own(k).wait_send()
    lax.fori_loop(1, n, settle_sums, 0)
    if helped:
        @pl.when(is_end)
        def _():
            send_up().wait_send()

        pl.when(is_aid)(settle_aid)
    over_steps(settle)


def cut(width, n, helped):
    if n > 8:
        return ((0, width),)
    tiles = width // 128
    first = max(1, tiles * 2 // 7) if helped else 0
    count = 4
    edges = [first + (tiles - first) * k // count for k in range(count + 1)]
    if helped:
        edges = [0] + edges
    return tuple((int(a * 128), int((b - a) * 128)) for a, b in zip(edges, edges[1:]))


def per_device(
    activations, rank_grads, lengths, adapter_ids, input_basis, rank_basis, prior_values
):
    n, own_n = lax.axis_size("blk"), lax.axis_size("own")
    tokens, width = activations.shape[1:]
    cols = input_basis.shape[0]
    share = cols // own_n
    seqs = lengths.shape[2]
    adapters, rank = rank_basis.shape[:2]
    lanes = seqs * adapters * rank
    helped = 4 <= n <= 8
    pieces = cut(width, n, helped)
    chunks = len(pieces)
    first = pieces[0][1] if helped else 128
    terms = 2 * seqs * rank
    vmem = pl.BlockSpec(memory_space=pltpu.VMEM)
    hbm = pl.BlockSpec(memory_space=pltpu.HBM)
    dma = pltpu.SemaphoreType.DMA
    f32 = jnp.float32
    sums = pl.pallas_call(
        functools.partial(kernel, n, own_n, pieces, helped),
        out_shape=jax.ShapeDtypeStruct((adapters, share, rank), f32),
        in_specs=[hbm] * 7,
        out_specs=vmem,
        scratch_shapes=[
            pltpu.SMEM(lengths.shape, jnp.int32),
            pltpu.SMEM(adapter_ids.shape, jnp.int32),
            pltpu.VMEM((1, rank, tokens), jnp.bfloat16),
            pltpu.VMEM(rank_basis.shape, f32),
            pltpu.VMEM((adapters, share, rank), f32),
            pltpu.VMEM((tokens, width), jnp.bfloat16),
            pltpu.VMEM((n, cols, width), jnp.bfloat16),
            pltpu.VMEM((n, cols, tokens), f32),
            pltpu.VMEM((n, own_n, share, lanes), f32),
            pltpu.VMEM((n, own_n, share, lanes), f32),
            dma((7,)),
            dma((n - 1, chunks)), dma((n - 1, chunks)),
            dma((n - 1, chunks)), dma((n - 1, chunks)),
            dma((n, own_n)), dma((n, own_n)),
            pltpu.VMEM((terms, first), jnp.bfloat16),
            pltpu.VMEM((terms, first), jnp.bfloat16),
            pltpu.VMEM((n if helped else 1, own_n, share, lanes), f32),
            pltpu.VMEM((2, own_n, share, lanes), f32),
            dma((2,)), dma((n, own_n)), dma((2, own_n)),
        ],
        compiler_params=pltpu.CompilerParams(
            collective_id=0, has_side_effects=True, vmem_limit_bytes=64 << 20
        ),
    )(
        lengths, adapter_ids, activations, jnp.transpose(rank_grads, (0, 2, 1)), input_basis,
        rank_basis, jnp.transpose(prior_values, (0, 2, 1)),
    )
    return jnp.transpose(sums, (0, 2, 1))


def solution(mesh):
    return jax.shard_map(
        per_device,
        mesh=mesh,
        in_specs=(
            P(None, ("group", "blk"), "own"),
            P(None, ("group", "blk"), None),
            P(None, ("group", "blk"), None),
            P(None, "group"),
            P(("group", "blk"), "own"),
            P("group", None, None),
            P("group", None, ("blk", "own")),
        ),
        out_specs=P("group", None, ("blk", "own")),
        check_vma=False,
    )
```
